128 devices in a mesh: dp: 4 (over y), expert: 32 (over x, z, core).
Axes of the slice: x: 4, y: 4, z: 4, core: 2. Of those that a mesh axis runs over, the one named last changes fastest.
Arguments:
- tokens: bfloat16 [32, 512, 2048], P('expert', 'dp'), may hold values from -6 to 6
- segment_ids: int32 [32, 512], P('expert', 'dp'), may hold values from 0 to 2, never falling along the last dimension, each value on 1 to 256 neighbouring positions
- routes: int32 [32, 512, 6], P('expert', 'dp'), may hold values from 0 to 63, all different within a row; in each aligned block of 128 rows (0 to 127, 128 to 255, ..., all dimensions but the last counted through in order) at most 16 rows name the same one
- norm_gain: float32 [2048], replicated, may hold values from 0.25 to 1.75
- w_query: bfloat16 [2048, 2048], P(None, 'dp')
- w_key: bfloat16 [2048, 512], P(None, 'dp')
- w_value: bfloat16 [2048, 512], P(None, 'dp'), may hold values from -0.125 to 0.125
- w_out: bfloat16 [2048, 2048], P('dp'), may hold values from -0.125 to 0.125
- ffn_gain: float32 [2048], replicated, may hold values from 0.25 to 1.75
- w_router: bfloat16 [2048, 64], replicated, may hold values from -0.125 to 0.125
- w_shared_gate: bfloat16 [2048, 2816], P(None, 'dp'), may hold values from -0.125 to 0.125
- w_shared_up: bfloat16 [2048, 2816], P(None, 'dp'), may hold values from -0.125 to 0.125
- w_shared_down: bfloat16 [2816, 2048], P('dp'), may hold values from -0.109375 to 0.109375
- w_expert_gate: bfloat16 [2048, 90112], P(None, ('dp', 'expert')), may hold values from -0.125 to 0.125
- w_expert_up: bfloat16 [2048, 90112], P(None, ('dp', 'expert')), may hold values from -0.125 to 0.125
- w_expert_down: bfloat16 [90112, 2048], P(('dp', 'expert')), may hold values from -0.15625 to 0.15625
Outputs:
- layer_out: bfloat16 [32, 512, 2048], P('expert', 'dp')
The draws below stay inside these ranges and needn't reach their ends.
Inputs may be any that keep to these rules, and one draw needn't show every extreme that they name: `routes`: each row names 6 different experts. In each aligned block of 128 rows (stream-major order; the rows of one device) no expert is named more than 16 times, a bound that some block reaches. `segment_ids`: along each stream ids never fall; each of the 3 prompts covers 1 to 256 tokens, one exactly 256.
All inputs are finite; a program needn't handle non-finite values.
Results may differ from the reference program's by a relative error of at most 0.02.
The reference program's roundings to bfloat16 on the way count: a program that leaves them out, or rounds other values in their place, can miss the bound.
Values may be sent and summed in bfloat16 or wider, within the bound.
A program may use at most 128 MiB of HBM per device.

```python
import math
import jax
import jax.numpy as jnp
import numpy as np
from jax import lax

D = 2048
HEADS = 16
KVH = 4
HD = 128
FFE = 1408
SFF = 2816
TOP = 6
TOK_DEV = 128
SEGS = 3
STREAMS = 32
GROUP = 512
SEG_MOST = 256
EXPERTS = 64
CAP = 16
N_DP = 4


def projection(key, heads):
    base = jax.random.truncated_normal(key, -6.0, 6.0, (D, heads * HD), jnp.float32) * D ** (-0.5)
    return base.astype(jnp.bfloat16)


def draw_w_query(key, part):
    return projection(jax.random.fold_in(key, 11), HEADS)


def draw_w_key(key, part):
    return projection(jax.random.fold_in(key, 13), KVH)


def levels(own_key, shape, pieces, low, high):
    factor_of, own = 1.0, jax.random.fold_in(own_key, 6)
    for position, blocks in pieces:
        steps = jnp.exp(jax.random.uniform(jax.random.fold_in(own, position), (blocks,), jnp.float32, low / len(pieces), high / len(pieces)))
        factor_of = factor_of * jnp.repeat(steps, shape[position] // blocks).reshape([-1 if axis == position else 1 for axis in range(len(shape))])
    return factor_of


def profile(amount, total, reach, skew):
    loads = [(1 << 20) // math.isqrt(standing ** skew) + 1 for standing in range(2, amount + 1)]
    surplus, counts = total - reach - (amount - 1), [1] * (amount - 1)
    while surplus > 0:
        free = [i for i in range(amount - 1) if counts[i] < reach]
        mass, left = sum([loads[i] for i in free]), surplus
        for i in free:
            more = min(reach - counts[i], max(1, left * loads[i] // mass), surplus)
            counts[i] = counts[i] + more
            surplus = surplus - more
    return np.array([reach] + counts)


def uneven(key, count, total, most, lean):
    if count == 2:
        one = jax.random.randint(key, (), max(1, total - most), min(most, total - 1) + 1)
        return jnp.stack([one, total - one])
    sizes = jnp.asarray(profile(count, total, most, lean), jnp.int32)
    couples = (count - 1) // 2
    giver, taker = sizes[1:1 + 2 * couples:2], sizes[2:2 + 2 * couples:2]
    margin = jnp.minimum(giver - 1, most - taker)
    passed = jax.random.randint(jax.random.fold_in(key, 1), (couples,), 0, 1 << 20) % (margin + 1)
    sizes = sizes.at[1:1 + 2 * couples:2].set(giver - passed).at[2:2 + 2 * couples:2].set(taker + passed)
    return sizes[jax.random.permutation(jax.random.fold_in(key, 2), count)]


def deal_out(rng, own, number, rows, count, top, bound, lean):
    order = jax.random.permutation(rng, count)
    heavy_load, ordinary = load_shares(count, rows * top, bound, lean, True), load_shares(count, rows * top, bound, lean, False)
    places = jnp.arange(count)

    def named(tallies, offset_by):
        used = int((tallies > 0).sum())
        fixed = max(1, used // 4)
        moved = fixed + (places - fixed + offset_by * (used - fixed)) % max(1, count - fixed)
        return jnp.zeros((count,), jnp.int32).at[order[jnp.where(places < fixed, places, moved)]].set(jnp.asarray(tallies, jnp.int32))

    tallies = jnp.where(number % 4 == 0, named(heavy_load, number // 4), named(ordinary, number - number // 4 - 1))
    mixed = jax.random.permutation(jax.random.fold_in(own, 3), count)
    donor, sink = mixed[0:count // 2 * 2:2], mixed[1:count // 2 * 2:2]
    slack = jnp.minimum(tallies[donor] - 1, bound - tallies[sink]) // 2
    slack = jnp.where((donor == order[0]) | (sink == order[0]) | (tallies[sink] == 0), 0, jnp.maximum(slack, 0))
    moved = jax.random.randint(jax.random.fold_in(own, 4), (count // 2,), 0, 1 << 20) % (slack + 1)
    tallies = tallies.at[donor].add(-moved).at[sink].add(moved)
    labels = jnp.searchsorted(jnp.cumsum(tallies), jnp.arange(rows * top), side="right").astype(jnp.int32)
    table = labels.reshape(top, rows).T
    table = table[jax.random.permutation(jax.random.fold_in(own, 1), rows)]
    offset_by = jax.random.randint(jax.random.fold_in(own, 2), (rows, 1), 0, top)
    return jnp.take_along_axis(table, (jnp.arange(top)[None, :] + offset_by) % top, axis=1)


def load_shares(count, total, most, lean, full):
    portions = [(1 << 20) // math.isqrt(rank ** lean) + 1 for rank in range(1, count + 1)]
    largest = most if full else min(most, max(-(-total // count), total * portions[0] // sum(portions)))
    least = 1 if total - largest >= count - 1 else 0
    given, spare = [largest] + [least] * (count - 1), total - largest - least * (count - 1)
    while spare > 0:
        free = [i for i in range(1, count) if given[i] < largest] or [i for i in range(1, count) if given[i] < most]
        whole, remaining = sum([portions[i] for i in free]), spare
        for i in free:
            extra = min(most - given[i], max(1, remaining * portions[i] // whole), spare)
            given[i] = given[i] + extra
            spare = spare - extra
    return np.array(given)


def centred(rng, shape, scale, reach, cuts=(), kind=jnp.bfloat16):
    array = jax.random.normal(rng, shape, jnp.float32) * scale
    if len(cuts) > 0:
        array = levels(rng, shape, cuts, -0.22, 0.18) * array
    return jnp.clip(array, min=-reach, max=reach).astype(kind)


def setup_inputs(seed: int = 0) -> dict:
    key_of = jax.random.split(jax.random.key(seed), 17)
    tokens = centred(key_of[0], (STREAMS, GROUP, D), 1.0, 6.0, ((0, 32), (1, 4)))
    segment_ids = jax.vmap(lambda own: jnp.searchsorted(jnp.cumsum(uneven(own, SEGS, GROUP, SEG_MOST, 2)), jnp.arange(GROUP), side="right"))(jax.random.split(key_of[1], STREAMS)).reshape((STREAMS, GROUP)).astype(jnp.int32)
    routes_keys = jax.random.split(jax.random.fold_in(key_of[2], 1), STREAMS * GROUP // TOK_DEV)
    routes_turns = jax.random.permutation(jax.random.fold_in(key_of[2], 3), STREAMS * GROUP // TOK_DEV)
    routes = jax.vmap(lambda own, number: deal_out(jax.random.fold_in(key_of[2], 2), own, number, TOK_DEV, EXPERTS, TOP, CAP, 1))(routes_keys, routes_turns).reshape((STREAMS, GROUP, TOP))
    norm_gain = jnp.clip(1.0 + 0.15 * jax.random.normal(key_of[3], (D,), jnp.float32), 0.25, 1.75)
    w_query = draw_w_query(jax.random.fold_in(key_of[16], 71), 0)
    w_key = draw_w_key(jax.random.fold_in(key_of[16], 71), 0)
    w_value = centred(key_of[6], (D, KVH * HD), D ** -0.5, 0.125, ((1, 4),))
    w_out = centred(key_of[7], (HEADS * HD, D), (HEADS * HD) ** -0.5, 0.125, ((0, 4),))
    ffn_gain = jnp.clip(1.0 + 0.15 * jax.random.normal(key_of[8], (D,), jnp.float32), 0.25, 1.75)
    w_router = centred(key_of[9], (D, EXPERTS), D ** -0.5, 0.125)
    w_shared_gate = centred(key_of[10], (D, SFF), D ** -0.5, 0.125, ((1, 4),))
    w_shared_up = centred(key_of[11], (D, SFF), D ** -0.5, 0.125, ((1, 4),))
    w_shared_down = centred(key_of[12], (SFF, D), SFF ** -0.5, 0.109375, ((0, 4),))
    w_expert_gate = centred(key_of[13], (D, EXPERTS * FFE), D ** -0.5, 0.125, ((1, 128),))
    w_expert_up = centred(key_of[14], (D, EXPERTS * FFE), D ** -0.5, 0.125, ((1, 128),))
    w_expert_down = centred(key_of[15], (EXPERTS * FFE, D), FFE ** -0.5, 0.15625, ((0, 128),))
    return {"tokens": tokens, "segment_ids": segment_ids, "routes": routes, "norm_gain": norm_gain, "w_query": w_query, "w_key": w_key, "w_value": w_value, "w_out": w_out, "ffn_gain": ffn_gain, "w_router": w_router, "w_shared_gate": w_shared_gate, "w_shared_up": w_shared_up, "w_shared_down": w_shared_down, "w_expert_gate": w_expert_gate, "w_expert_up": w_expert_up, "w_expert_down": w_expert_down}


epsilon = 1e-06

def rms_norm(values, gain):
    wide = values.astype(jnp.float32)
    scale = lax.rsqrt(lax.optimization_barrier(jnp.mean(wide * wide, axis=-1, keepdims=True)) + epsilon)
    return (wide * scale * gain.astype(jnp.float32)).astype(jnp.bfloat16)

def positions(segment):
    count = segment.shape[0]
    index = jnp.arange(count, dtype=jnp.int32)
    same = (segment[:, None] == segment[None, :]) & (index[None, :] < index[:, None])
    return lax.optimization_barrier(jnp.sum(same.astype(jnp.int32), axis=1))

def rotate(heads, place):
    half = heads.shape[-1] // 2
    freq = 10000.0 ** (-jnp.arange(half, dtype=jnp.float32) / half)
    angle = place.astype(jnp.float32)[:, None] * freq[None, :]
    cosine = jnp.cos(angle)[:, None, :]
    sine = jnp.sin(angle)[:, None, :]
    first = heads[..., :half]
    second = heads[..., half:]
    return jnp.concatenate([first * cosine - second * sine, second * cosine + first * sine], axis=-1)

def attend(normed, segment, w_query, w_key, w_value):
    rows = normed.shape[0]
    query_heads = w_query.shape[1] // HD
    value_heads = w_key.shape[1] // HD
    group_size = query_heads // value_heads
    place = positions(segment)
    query = jnp.dot(normed, w_query, preferred_element_type=jnp.float32).reshape(rows, query_heads, HD)
    query = rotate(query, place).astype(jnp.bfloat16).reshape(rows, value_heads, group_size, HD)
    keyed = jnp.dot(normed, w_key, preferred_element_type=jnp.float32).reshape(rows, value_heads, HD)
    keyed = rotate(keyed, place).astype(jnp.bfloat16)
    valued = jnp.dot(normed, w_value, preferred_element_type=jnp.float32).astype(jnp.bfloat16).reshape(rows, value_heads, HD)
    block = min(rows, 512)
    index = jnp.arange(rows, dtype=jnp.int32)

    def one_block(start):
        query_block = lax.dynamic_slice_in_dim(query, start, block, 0)
        segment_block = lax.dynamic_slice_in_dim(segment, start, block, 0)
        index_block = start + jnp.arange(block, dtype=jnp.int32)
        scores = jnp.einsum('qkgd,skd->kgqs', query_block.astype(jnp.float32), keyed.astype(jnp.float32)) * HD ** (-0.5)
        allowed = (segment_block[:, None] == segment[None, :]) & (index[None, :] <= index_block[:, None])
        scores = jnp.where(allowed[None, None], scores, -1e+30)
        highest = lax.optimization_barrier(jnp.max(scores, axis=-1, keepdims=True))
        expo = jnp.exp(scores - highest)
        weights = (expo / lax.optimization_barrier(jnp.sum(expo, axis=-1, keepdims=True))).astype(jnp.bfloat16)
        mixed = jnp.einsum('kgqs,skd->qkgd', weights.astype(jnp.float32), valued.astype(jnp.float32))
        return mixed.astype(jnp.bfloat16).reshape(block, query_heads * HD)
    starts = jnp.arange(rows // block, dtype=jnp.int32) * block
    return lax.map(one_block, starts).reshape(rows, query_heads * HD)

def rounded(values):
    return lax.optimization_barrier(values.astype(jnp.bfloat16)).astype(jnp.float32)

def route_gates(logits, route):
    chosen = jnp.take_along_axis(logits, route, axis=1)
    highest = lax.optimization_barrier(jnp.max(chosen, axis=1, keepdims=True))
    expo = jnp.exp(chosen - highest)
    return expo / lax.optimization_barrier(jnp.sum(expo, axis=1, keepdims=True))

def reference(tokens, segment_ids, routes, norm_gain, w_query, w_key, w_value, w_out, ffn_gain, w_router, w_shared_gate, w_shared_up, w_shared_down, w_expert_gate, w_expert_up, w_expert_down):
    width = tokens.shape[2]
    head_width = w_out.shape[0] // N_DP
    shared_width = w_shared_down.shape[0] // N_DP
    expert_count = w_router.shape[1]

    def stream_part(inputs):
        rows, segment, route = inputs
        normed = rms_norm(rows, norm_gain)
        attended = attend(normed, segment, w_query, w_key, w_value)
        head_sum = jnp.zeros((rows.shape[0], width), jnp.float32)
        for block in range(N_DP):
            part = jnp.dot(attended[:, block * head_width:(block + 1) * head_width], w_out[block * head_width:(block + 1) * head_width], preferred_element_type=jnp.float32)
            head_sum = head_sum + rounded(part)
        residual = (rows.astype(jnp.float32) + head_sum).astype(jnp.bfloat16)
        mixed = rms_norm(residual, ffn_gain)
        hidden = (jax.nn.silu(jnp.dot(mixed, w_shared_gate, preferred_element_type=jnp.float32)) * jnp.dot(mixed, w_shared_up, preferred_element_type=jnp.float32)).astype(jnp.bfloat16)
        shared_sum = jnp.zeros((rows.shape[0], width), jnp.float32)
        for block in range(N_DP):
            part = jnp.dot(hidden[:, block * shared_width:(block + 1) * shared_width], w_shared_down[block * shared_width:(block + 1) * shared_width], preferred_element_type=jnp.float32)
            shared_sum = shared_sum + rounded(part)
        logits = jnp.dot(mixed, w_router, preferred_element_type=jnp.float32)
        gates = route_gates(logits, route)
        return (residual, shared_sum, mixed, gates)
    residual, shared_sum, mixed, gates = lax.map(stream_part, (tokens, segment_ids, routes))
    total_tokens = tokens.shape[0] * tokens.shape[1]
    blocks = total_tokens // TOK_DEV
    capacity = 4 * TOK_DEV * TOP // (3 * expert_count)
    total_routes = total_tokens * TOP
    flat_routes = routes.reshape(blocks, TOK_DEV * TOP)
    onehot = (flat_routes[:, :, None] == jnp.arange(expert_count, dtype=jnp.int32)[None, None, :]).astype(jnp.int32)
    slot = lax.optimization_barrier(jnp.sum(jnp.cumsum(onehot, axis=1) * onehot, axis=2)) - 1
    route_id = jnp.arange(total_routes, dtype=jnp.int32).reshape(blocks, TOK_DEV * TOP)
    block_id = jnp.broadcast_to(jnp.arange(blocks, dtype=jnp.int32)[:, None], (blocks, TOK_DEV * TOP))
    table = jnp.full((expert_count, blocks, capacity), total_routes, jnp.int32).at[flat_routes, block_id, slot].set(route_id)
    mixed_flat = mixed.reshape(total_tokens, width)
    gates_flat = gates.reshape(total_routes)
    half = FFE // 2

    def expert_step(carry, expert):
        ids = table[expert].reshape(-1)
        valid = ids < total_routes
        safe = jnp.where(valid, ids, 0)
        token = safe // TOP
        rows = jnp.where(valid[:, None], mixed_flat[token], jnp.zeros((), jnp.bfloat16)).astype(jnp.bfloat16)
        total = jnp.zeros((rows.shape[0], width), jnp.float32)
        for side in range(2):
            column = (expert * FFE + side * half).astype(jnp.int32)
            gate_cols = lax.dynamic_slice_in_dim(w_expert_gate, column, half, 1)
            up_cols = lax.dynamic_slice_in_dim(w_expert_up, column, half, 1)
            down_rows = lax.dynamic_slice_in_dim(w_expert_down, column, half, 0)
            active = (jax.nn.silu(jnp.dot(rows, gate_cols, preferred_element_type=jnp.float32)) * jnp.dot(rows, up_cols, preferred_element_type=jnp.float32)).astype(jnp.bfloat16)
            total = total + rounded(jnp.dot(active, down_rows, preferred_element_type=jnp.float32))
        output = rounded(total)
        term = jnp.where(valid[:, None], gates_flat[safe][:, None] * output, 0.0)
        return (carry.at[token].add(term), None)
    routed, unused = lax.scan(expert_step, jnp.zeros((total_tokens, width), jnp.float32), jnp.arange(expert_count, dtype=jnp.int32))
    routed = routed.reshape(tokens.shape)
    return (residual.astype(jnp.float32) + shared_sum + routed).astype(jnp.bfloat16)
```

```python
import jax
import jax.numpy as jnp
from jax import lax
from jax.experimental import pallas as pl
from jax.experimental.pallas import tpu as pltpu
from jax.sharding import PartitionSpec as P

HD = 128
TOP = 6
WIDTH = 2048
TOK = 128
HID = 704
CAP = 16
MESH = pl.DeviceIdType.MESH
ANY = pl.BlockSpec(memory_space=pl.ANY)
VMEM = pl.BlockSpec(memory_space=pltpu.VMEM)
COLS = ((0, 256), (256, 256), (512, 192))

epsilon = 1e-06


def rms_norm(values, gain):
    wide = values.astype(jnp.float32)
    scale = lax.rsqrt(jnp.mean(wide * wide, axis=-1, keepdims=True) + epsilon)
    return (wide * scale * gain).astype(jnp.bfloat16)


def positions(segment):
    count = segment.shape[0]
    index = jnp.arange(count, dtype=jnp.int32)
    same = (segment[:, None] == segment[None, :]) & (index[None, :] < index[:, None])
    return jnp.sum(same.astype(jnp.int32), axis=1)


def rotate(heads, place):
    half = heads.shape[-1] // 2
    freq = 10000.0 ** (-jnp.arange(half, dtype=jnp.float32) / half)
    angle = place.astype(jnp.float32)[:, None] * freq[None, :]
    cosine = jnp.cos(angle)[:, None, :]
    sine = jnp.sin(angle)[:, None, :]
    first = heads[..., :half]
    second = heads[..., half:]
    return jnp.concatenate(
        [first * cosine - second * sine, second * cosine + first * sine], axis=-1
    )


def attend(normed, segment, w_query, w_key, w_value):
    rows = normed.shape[0]
    query_heads = w_query.shape[1] // HD
    value_heads = w_key.shape[1] // HD
    group_size = query_heads // value_heads
    place = positions(segment)
    query = jnp.dot(normed, w_query, preferred_element_type=jnp.float32).reshape(
        rows, query_heads, HD
    )
    query = rotate(query, place).astype(jnp.bfloat16).reshape(rows, value_heads, group_size, HD)
    keyed = jnp.dot(normed, w_key, preferred_element_type=jnp.float32).reshape(
        rows, value_heads, HD
    )
    keyed = rotate(keyed, place).astype(jnp.bfloat16)
    valued = (
        jnp.dot(normed, w_value, preferred_element_type=jnp.float32)
        .astype(jnp.bfloat16)
        .reshape(rows, value_heads, HD)
    )
    index = jnp.arange(rows, dtype=jnp.int32)
    scores = jnp.einsum("qkgd,skd->kgqs", query, keyed, preferred_element_type=jnp.float32) * HD ** (
        -0.5
    )
    allowed = (segment[:, None] == segment[None, :]) & (index[None, :] <= index[:, None])
    scores = jnp.where(allowed[None, None], scores, -1e30)
    highest = jnp.max(scores, axis=-1, keepdims=True)
    expo = jnp.exp(scores - highest)
    weights = (expo / jnp.sum(expo, axis=-1, keepdims=True)).astype(jnp.bfloat16)
    mixed = jnp.einsum("kgqs,skd->qkgd", weights, valued, preferred_element_type=jnp.float32)
    return mixed.astype(jnp.bfloat16).reshape(rows, query_heads * HD)


def dot(a, b):
    return jnp.dot(a, b, preferred_element_type=jnp.float32)


def moe_kernel(
    mixed_ref,
    residual_ref,
    pick_ref,
    place_ref,
    named_ref,
    router_ref,
    eg_hbm,
    eu_hbm,
    ed_hbm,
    sg_hbm,
    su_hbm,
    sd_hbm,
    out_ref,
    eg,
    eu,
    ed,
    sg,
    su,
    sd,
    blocks,
    send,
    recv,
    half,
    mate,
    back,
    part,
    gather,
    act,
    hidden,
    gate_hi,
    gate_lo,
    weight_sem,
    block_send,
    block_recv,
    send_sem,
    recv_sem,
    fwd_send,
    fwd_recv,
    mate_send,
    mate_recv,
    back_send,
    back_recv,
    part_send,
    part_recv,
):
    y = lax.axis_index("dp")
    place = lax.axis_index("expert")
    chip = place // 2
    core = place % 2
    other = 1 - core
    weights = (
        (eg_hbm, eg),
        (eu_hbm, eu),
        (ed_hbm, ed),
        (sg_hbm, sg),
        (su_hbm, su),
        (sd_hbm, sd),
    )
    for i, (src, dst) in enumerate(weights):
        pltpu.make_async_copy(src, dst, weight_sem.at[i]).start()

    def wait_weights(first, last):
        for i in range(first, last):
            pltpu.make_async_copy(weights[i][0], weights[i][1], weight_sem.at[i]).wait()

    def peer(i):
        target = (chip + i) % 16
        return target, (y, target * 2 + core)

    sibling = (y, chip * 2 + other)

    barrier = pltpu.get_barrier_semaphore()
    for step in range(1, 4):
        pl.semaphore_signal(
            barrier, inc=1, device_id=((y + step) % 4, place), device_id_type=MESH
        )
    pl.semaphore_signal(barrier, inc=1, device_id=sibling, device_id_type=MESH)

    def greet(i, carry):
        pl.semaphore_signal(barrier, inc=1, device_id=peer(i)[1], device_id_type=MESH)
        return carry

    lax.fori_loop(1, 16, greet, 0)
    pl.semaphore_wait(barrier, 19)

    def share(slot, step):
        return pltpu.make_async_remote_copy(
            src_ref=mixed_ref,
            dst_ref=blocks.at[slot],
            send_sem=block_send.at[slot],
            recv_sem=block_recv.at[slot],
            device_id=((y + step) % 4, place),
            device_id_type=MESH,
        )

    shares = {1: share(1, 1), 2: share(2, 3), 3: share(3, 2)}
    shares[1].start()
    shares[2].start()
    blocks[0] = mixed_ref[...]

    def scatter(source, target, sends, recvs, i):
        def one(k, carry):
            to, device = peer(k)
            pltpu.make_async_remote_copy(
                src_ref=source.at[pl.ds(pl.multiple_of(to * CAP, CAP), CAP)],
                dst_ref=target.at[pl.ds(pl.multiple_of(chip * CAP, CAP), CAP)],
                send_sem=sends.at[i],
                recv_sem=recvs.at[i],
                device_id=device,
                device_id_type=MESH,
            ).start()
            return carry

        lax.fori_loop(1, 16, one, 0)
        own = pl.ds(pl.multiple_of(chip * CAP, CAP), CAP)
        pltpu.make_async_copy(source.at[own], target.at[own], recvs.at[i]).start()

    def wait_rows(ref, sem, rows):
        view = ref.at[pl.ds(0, rows)]
        pltpu.make_async_copy(view, view, sem).wait()

    def dispatch(i):
        def columns(n, carry):
            cols = pl.ds(pl.multiple_of(n * 512, 512), 512)
            send[i, :, cols] = dot(pick_ref[i], blocks[i, :, cols]).astype(jnp.bfloat16)
            return carry

        lax.fori_loop(0, 4, columns, 0)
        scatter(send.at[i], recv.at[i, core], send_sem, recv_sem, i)

    def activate(rows, wg, wu, target):
        for start, size in COLS:
            gated = dot(rows, wg[:, start : start + size])
            lifted = dot(rows, wu[:, start : start + size])
            target[:, start : start + size] = (
                gated / (1.0 + jnp.exp(-gated)) * lifted
            ).astype(jnp.bfloat16)

    def shared_hidden(i):
        activate(blocks[i], sg, su, hidden.at[i])

    def gates(i):
        logits = dot(blocks[i], router_ref[...])
        named = named_ref[i] > 0.5
        highest = jnp.max(jnp.where(named, logits, -jnp.inf), axis=1, keepdims=True)
        expo = jnp.where(named, jnp.exp(jnp.where(named, logits, highest) - highest), 0.0)
        gate = expo / jnp.sum(expo, axis=1, keepdims=True)
        high = gate.astype(jnp.bfloat16)
        low = (gate - high.astype(jnp.float32)).astype(jnp.bfloat16)
        row = lax.broadcasted_iota(jnp.int32, (64, 16 * CAP), 0)
        column = lax.broadcasted_iota(jnp.int32, (64, 16 * CAP), 1)
        spread = jnp.where(row == column // CAP + 16 * y, 1.0, 0.0).astype(jnp.bfloat16)
        placed = place_ref[i].astype(jnp.float32)
        gate_hi[i] = (dot(high, spread) * placed).astype(jnp.bfloat16)
        gate_lo[i] = (dot(low, spread) * placed).astype(jnp.bfloat16)

    def forward(i):
        return pltpu.make_async_remote_copy(
            src_ref=recv.at[i, core],
            dst_ref=recv.at[i, core],
            send_sem=fwd_send.at[i],
            recv_sem=fwd_recv.at[i],
            device_id=sibling,
            device_id_type=MESH,
        )

    def to_mate(i):
        return pltpu.make_async_remote_copy(
            src_ref=half.at[i, 1],
            dst_ref=mate.at[i],
            send_sem=mate_send.at[i],
            recv_sem=mate_recv.at[i],
            device_id=sibling,
            device_id_type=MESH,
        )

    def experts(i):
        def side(j, carry):
            which = (core + j) % 2

            @pl.when(j == 0)
            def _():
                wait_rows(recv.at[i, core], recv_sem.at[i], 256)
                forward(i).start()

            @pl.when(j == 1)
            def _():
                wait_rows(recv.at[i, other], fwd_recv.at[i], 256)

            activate(recv[i, which], eg, eu, act)

            def columns(n, carry):
                cols = pl.ds(pl.multiple_of(n * 512, 512), 512)
                half[i, j, :, cols] = dot(act[...], ed[:, cols]).astype(jnp.bfloat16)
                return carry

            lax.fori_loop(0, 4, columns, 0)

            @pl.when(j == 1)
            def _():
                to_mate(i).start()

            return carry

        lax.fori_loop(0, 2, side, 0)

    def give_back(i):
        wait_rows(mate.at[i], mate_recv.at[i], 256)

        def rows(n, carry):
            r = pl.ds(pl.multiple_of(n * 32, 32), 32)
            half[i, 0, r, :] = (
                half[i, 0, r, :].astype(jnp.float32) + mate[i, r, :].astype(jnp.float32)
            ).astype(jnp.bfloat16)
            return carry

        lax.fori_loop(0, 8, rows, 0)
        scatter(half.at[i, 0], back.at[i], back_send, back_recv, i)

    dispatch(0)
    gates(0)
    wait_weights(3, 6)
    shared_hidden(0)
    shares[1].wait_send()
    shares[2].wait_send()
    shares[3].start()
    shares[1].wait_recv()
    dispatch(1)
    shares[2].wait_recv()
    dispatch(2)
    wait_weights(0, 3)

    def stage(i, carry):
        experts(i)

        @pl.when(i == 0)
        def _():
            shares[3].wait_recv()
            dispatch(3)

            def others(k, carry):
                gates(k)
                shared_hidden(k)
                return carry

            lax.fori_loop(1, 4, others, 0)

        @pl.when(i > 0)
        def _():
            give_back(i)

        return carry

    lax.fori_loop(0, 4, stage, 0)
    give_back(0)

    def combine(i, store):
        wait_rows(back.at[i], back_recv.at[i], 256)

        def columns(n, carry):
            cols = pl.ds(pl.multiple_of(n * 512, 512), 512)
            rows = back[i, :, cols]
            store(
                cols,
                dot(gate_hi[i], rows) + dot(gate_lo[i], rows) + dot(hidden[i], sd[:, cols]),
            )
            return carry

        lax.fori_loop(0, 4, columns, 0)

    def part_copy(i, step):
        return pltpu.make_async_remote_copy(
            src_ref=part.at[i - 1],
            dst_ref=gather.at[i - 1],
            send_sem=part_send.at[i - 1],
            recv_sem=part_recv.at[i - 1],
            device_id=((y + step) % 4, place),
            device_id_type=MESH,
        )

    parts = {1: part_copy(1, 3), 2: part_copy(2, 1), 3: part_copy(3, 2)}

    def remote_part(i, carry):
        def store(cols, total):
            part[i - 1, :, cols] = total.astype(jnp.bfloat16)

        combine(i, store)
        for k in (1, 2, 3):

            @pl.when(i == k)
            def _(k=k):
                parts[k].start()

        return carry

    lax.fori_loop(1, 4, remote_part, 0)
    for k in (1, 2, 3):
        parts[k].wait_recv()

    def store_own(cols, total):
        for k in range(3):
            total = total + gather[k, :, cols].astype(jnp.float32)
        total = total + residual_ref[:, cols].astype(jnp.float32)
        out_ref[:, cols] = total.astype(jnp.bfloat16)

    combine(0, store_own)

    shares[3].wait_send()
    for k in (1, 2, 3):
        parts[k].wait_send()

    def drain(i, carry):
        wait_rows(send.at[i], send_sem.at[i], 240)
        wait_rows(half.at[i, 0], back_send.at[i], 240)
        wait_rows(recv.at[i, core], fwd_send.at[i], 256)
        wait_rows(half.at[i, 1], mate_send.at[i], 256)
        return carry

    lax.fori_loop(0, 4, drain, 0)


def moe(mixed, residual, pick, place, named, w_router, weights):
    bf16 = jnp.bfloat16
    scratch = [
        pltpu.VMEM((WIDTH, HID), bf16),
        pltpu.VMEM((WIDTH, HID), bf16),
        pltpu.VMEM((HID, WIDTH), bf16),
        pltpu.VMEM((WIDTH, HID), bf16),
        pltpu.VMEM((WIDTH, HID), bf16),
        pltpu.VMEM((HID, WIDTH), bf16),
        pltpu.VMEM((4, TOK, WIDTH), bf16),
        pltpu.VMEM((4, 256, WIDTH), bf16),
        pltpu.VMEM((4, 2, 256, WIDTH), bf16),
        pltpu.VMEM((4, 2, 256, WIDTH), bf16),
        pltpu.VMEM((4, 256, WIDTH), bf16),
        pltpu.VMEM((4, 256, WIDTH), bf16),
        pltpu.VMEM((3, TOK, WIDTH), bf16),
        pltpu.VMEM((3, TOK, WIDTH), bf16),
        pltpu.VMEM((256, HID), bf16),
        pltpu.VMEM((4, TOK, HID), bf16),
        pltpu.VMEM((4, TOK, 256), bf16),
        pltpu.VMEM((4, TOK, 256), bf16),
        pltpu.SemaphoreType.DMA((6,)),
        pltpu.SemaphoreType.DMA((4,)),
        pltpu.SemaphoreType.DMA((4,)),
    ] + [pltpu.SemaphoreType.DMA((4,))] * 10
    return pl.pallas_call(
        moe_kernel,
        name="moe",
        out_shape=jax.ShapeDtypeStruct((TOK, WIDTH), bf16),
        in_specs=[VMEM] * 6 + [ANY] * 6,
        out_specs=VMEM,
        scratch_shapes=scratch,
        compiler_params=pltpu.CompilerParams(
            collective_id=1, has_side_effects=True, vmem_limit_bytes=63_000_000
        ),
        cost_estimate=pl.CostEstimate(
            flops=24_000_000_000, bytes_accessed=20_000_000, transcendentals=2_000_000
        ),
    )(mixed, residual, pick, place, named, w_router, *weights)


def per_device(
    tokens,
    segment_ids,
    routes,
    norm_gain,
    w_query,
    w_key,
    w_value,
    w_out,
    ffn_gain,
    w_router,
    w_shared_gate,
    w_shared_up,
    w_shared_down,
    w_expert_gate,
    w_expert_up,
    w_expert_down,
):
    own_rows = tokens[0]
    normed = rms_norm(own_rows, norm_gain)
    group_rows = lax.all_gather(normed, "dp", axis=0, tiled=True)
    packed = jnp.concatenate([routes[0], segment_ids[0][:, None]], axis=1)
    packed = lax.all_gather(packed, "dp", axis=0, tiled=True)
    group_routes = packed[:, :TOP]
    group_segments = packed[:, TOP]
    y = lax.axis_index("dp")
    labels = jnp.arange(64, dtype=jnp.int32)
    named = jnp.any(group_routes[:, :, None] == labels, axis=1).astype(jnp.bfloat16)
    named = named.reshape(4, TOK, 64)
    named = jnp.stack(
        [
            lax.dynamic_index_in_dim(named, (y + step) % 4, 0, keepdims=False)
            for step in (0, 3, 1, 2)
        ]
    )
    before = jnp.tril(jnp.ones((TOK, TOK), jnp.bfloat16), -1)
    slot = jnp.einsum("st,bte->bse", before, named, preferred_element_type=jnp.float32)
    named_here = lax.dynamic_slice_in_dim(named, 16 * y, 16, 2)
    slot_here = lax.dynamic_slice_in_dim(slot, 16 * y, 16, 2)
    slots = jnp.arange(CAP, dtype=jnp.float32)
    place = (
        (named_here[..., None] > 0.5) & (slot_here[..., None] == slots)
    ).astype(jnp.bfloat16).reshape(4, TOK, 256)
    pick = place.transpose(0, 2, 1)

    attended = attend(group_rows, group_segments, w_query, w_key, w_value)
    head_sum = lax.psum_scatter(
        jnp.dot(attended, w_out, preferred_element_type=jnp.float32).astype(jnp.bfloat16),
        "dp",
        scatter_dimension=0,
        tiled=True,
    ).astype(jnp.float32)
    residual = (own_rows.astype(jnp.float32) + head_sum).astype(jnp.bfloat16)
    mixed = rms_norm(residual, ffn_gain)
    output = moe(
        mixed,
        residual,
        pick,
        place,
        named.astype(jnp.float32),
        w_router,
        (
            w_expert_gate,
            w_expert_up,
            w_expert_down,
            w_shared_gate,
            w_shared_up,
            w_shared_down,
        ),
    )
    return output[None]


def solution(mesh):
    in_specs = (
        P("expert", "dp", None),
        P("expert", "dp"),
        P("expert", "dp", None),
        P(),
        P(None, "dp"),
        P(None, "dp"),
        P(None, "dp"),
        P("dp", None),
        P(),
        P(),
        P(None, "dp"),
        P(None, "dp"),
        P("dp", None),
        P(None, ("dp", "expert")),
        P(None, ("dp", "expert")),
        P(("dp", "expert"), None),
    )
    out_specs = P("expert", "dp", None)
    return jax.shard_map(
        per_device, mesh=mesh, in_specs=in_specs, out_specs=out_specs, check_vma=False
    )
```
